128 devices in a mesh: sec: 16 (over z, y), mpo: 8 (over x, core).
Axes of the slice: x: 4, y: 4, z: 4, core: 2. Of those that a mesh axis runs over, the one named last changes fastest.
Arguments:
- psi: bfloat16 [256, 8, 64, 128], P('sec'), may hold values from -6 to 6
- left_env: bfloat16 [32, 256, 64, 64], P('mpo', 'sec'), may hold values from -0.125 to 0.125
- right_env: bfloat16 [32, 256, 128, 128], P('mpo', 'sec'), may hold values from -0.5 to 0.5
- source: int32 [32, 256], P('mpo', 'sec'), may hold values from 0 to 255, as said below
- active: int32 [32, 256], P('mpo', 'sec'), may hold values 0 or 1
Outputs:
- h_psi: bfloat16 [256, 8, 64, 128], P('sec', 'mpo')
The draws below stay inside these ranges and needn't reach their ends.
Inputs may be any that keep to these rules, and one draw needn't show every extreme that they name: `source`: among the 4 x 16 entries of each aligned block (MPO indices w0 * 4 onward, sectors s0 * 16 onward), at most 8 name sectors of any one aligned group of 16 sectors, and exactly 8 name sectors of the block's own group s0.
All inputs are finite; a program needn't handle non-finite values. No bound on the sum of `active` on one device may be relied on, other than what follows from the above.
Results may differ from the reference program's by a relative error of at most 0.0049.
Values may be sent and summed in bfloat16 or wider, within the bound.
No kernel may reach another device: no remote copies, remote signals or barrier semaphores. Data moves between devices by JAX's collectives and lax.ppermute only.
A program may use at most 128 MiB of HBM per device.

```python
import jax
import jax.numpy as jnp
from jax import lax

SEC_DEV = 16
W_DEV = 4
NV = 8
DL = 64
DR = 128
CAP = 8
SECTORS = 256
MPOB = 32
N_SEC = 16
N_MPO = 8


def draw_source(key, part):
    key = jax.random.fold_in(key, 7)
    pair_count = W_DEV * SEC_DEV

    def block_map(block_key, home):
        key_one, key_two, key_three = jax.random.split(block_key, 3)
        others = jnp.arange((N_SEC - 1) * CAP, dtype=jnp.int32) // CAP
        others = others + (others >= home).astype(jnp.int32)
        picked = jax.random.permutation(key_one, others)[:pair_count - CAP]
        owners = jnp.concatenate([jnp.full((CAP,), home, jnp.int32), picked])
        owners = jax.random.permutation(key_two, owners)
        within = jax.random.randint(key_three, (pair_count,), 0, SEC_DEV, dtype=jnp.int32)
        return (owners * SEC_DEV + within).reshape(W_DEV, SEC_DEV)
    block_keys = jax.random.split(key, N_MPO * N_SEC)
    homes = jnp.tile(jnp.arange(N_SEC, dtype=jnp.int32), N_MPO)
    blocks = jax.vmap(block_map)(block_keys, homes)
    blocks = blocks.reshape(N_MPO, N_SEC, W_DEV, SEC_DEV).transpose(0, 2, 1, 3)
    return blocks.reshape(W_DEV * N_MPO, SEC_DEV * N_SEC).astype(jnp.int32)


def set_ends(drawn, stream_key, low, largest):
    extent = drawn.shape
    index_at = [jax.random.randint(jax.random.fold_in(stream_key, axis), (), 0, extent[axis]) for axis in range(len(extent))]
    drawn = drawn.at[tuple(index_at)].set(low)
    longest = extent.index(max(extent))
    index_at[longest] = (index_at[longest] + 1) % extent[longest]
    return drawn.at[tuple(index_at)].set(largest)


def block_scale(key, dims, cuts, least, top_value):
    gain, own = 1.0, jax.random.fold_in(key, 6)
    for position, blocks in cuts:
        steps = jnp.exp(jax.random.uniform(jax.random.fold_in(own, position), (blocks,), jnp.float32, least / len(cuts), top_value / len(cuts)))
        gain = gain * jnp.repeat(steps, dims[position] // blocks).reshape([-1 if axis == position else 1 for axis in range(len(dims))])
    return gain


def normal_values(own_key, extent, spread, most, cuts=(), held_as=jnp.bfloat16):
    entries = spread * jax.random.normal(own_key, extent, jnp.float32)
    if cuts:
        entries = entries * block_scale(own_key, extent, cuts, -0.22, 0.18)
    return jnp.clip(entries, -most, most).astype(held_as)


def setup_inputs(seed: int = 0) -> dict:
    arg_keys = jax.random.split(jax.random.key(seed), 6)
    return {
        "psi": normal_values(arg_keys[0], (SECTORS, NV, DL, DR), 1.0, 6.0, ((0, 16),)),
        "left_env": normal_values(arg_keys[1], (MPOB, SECTORS, DL, DL), (DL * MPOB) ** -0.5, 0.125, ((0, 8), (1, 16))),
        "right_env": normal_values(arg_keys[2], (MPOB, SECTORS, DR, DR), DR ** -0.5, 0.5, ((0, 8), (1, 16))),
        "source": draw_source(jax.random.fold_in(arg_keys[5], 71), 0),
        "active": set_ends((jax.random.randint(arg_keys[4], (MPOB, SECTORS), 0, 4) < 3).astype(jnp.int32), jax.random.fold_in(arg_keys[4], 1), 0, 1),
    }


def reference(psi, left_env, right_env, source, active):
    def sector_term(sector):
        blocks = jnp.take(psi, source[:, sector], axis=0).astype(jnp.float32)
        left_block = left_env[:, sector].astype(jnp.float32)
        right_block = right_env[:, sector].astype(jnp.float32)
        applied = jnp.einsum("wab,wvbc->wvac", left_block, blocks).astype(jnp.bfloat16)
        applied = lax.optimization_barrier(applied).astype(jnp.float32)
        result = jnp.einsum("wvac,wcd->wvad", applied, right_block)
        weights = active[:, sector].astype(jnp.float32)
        return jnp.sum(result * weights[:, None, None, None], axis=0)

    summed = lax.map(sector_term, jnp.arange(SECTORS))
    return summed.astype(jnp.bfloat16)
```

```python
import jax
import jax.numpy as jnp
from jax import lax
from jax.experimental import pallas as pl
from jax.experimental.pallas import tpu as pltpu
from jax.sharding import PartitionSpec as P

SIDE = 4
N_MPO = 8
BF = jnp.bfloat16
F32 = jnp.float32


def mpo_perm(fn):
    return [(m, fn(m)) for m in range(N_MPO)]


CORE = mpo_perm(lambda m: m ^ 1)
FAR = mpo_perm(lambda m: m ^ 4)
X_UP = mpo_perm(lambda m: (m + 2) % N_MPO)
X_DOWN = mpo_perm(lambda m: (m - 2) % N_MPO)


def ring_perm(first, step):
    pairs = []
    for z in range(SIDE):
        for y in range(SIDE):
            for m in range(N_MPO):
                if (m % 2 == 0) == first:
                    to = ((z + step) % SIDE) * SIDE + y
                else:
                    to = z * SIDE + (y + step) % SIDE
                pairs.append(((z * SIDE + y) * N_MPO + m, to * N_MPO + m))
    return pairs


A_UP, A_DOWN = ring_perm(True, 1), ring_perm(True, -1)
B_UP, B_DOWN = ring_perm(False, 1), ring_perm(False, -1)


def over_all(x, perm):
    return lax.ppermute(x, ("sec", "mpo"), perm)


def over_mpo(x, perm):
    return lax.ppermute(x, "mpo", perm)


def slot_of(t):
    return jnp.where(t == 0, 0, jnp.where(t == 3, 1, jnp.where(t == 1, 2, 3)))


def kernel(code_ref, c_ref, p_ref, n_ref, f0, f1, o0, o1, *refs):
    l_refs, r_refs, (out_ref, psi, sems) = refs[:4], refs[4:8], refs[8:]
    s = pl.program_id(0)
    sec = psi.shape[2]

    @pl.when(s == 0)
    def _():
        copies = [
            pltpu.make_async_copy(c_ref, psi.at[:, 0:4], sems.at[0]),
            pltpu.make_async_copy(p_ref, psi.at[:, 4:8], sems.at[1]),
            pltpu.make_async_copy(n_ref, psi.at[:, 8:12], sems.at[2]),
            pltpu.make_async_copy(f0, psi.at[0, 12:14], sems.at[3]),
            pltpu.make_async_copy(f1, psi.at[0, 14:16], sems.at[4]),
            pltpu.make_async_copy(o0, psi.at[1, 12:14], sems.at[5]),
            pltpu.make_async_copy(o1, psi.at[1, 14:16], sems.at[6]),
        ]
        for copy in copies:
            copy.start()
        for copy in copies:
            copy.wait()

    applied = []
    for g in range(4):
        for w in range(4):
            code = code_ref[g, w, s]
            at = jnp.maximum(code, 0)
            slot, row = at // sec, at % sec
            keep = jnp.where(code >= 0, 1.0, 0.0)
            packed = l_refs[g][w, 0]
            half = packed.shape[1] // 2
            left = jnp.concatenate([packed[:, :half], packed[:, half:]], axis=0)
            block = jnp.concatenate([psi[0, slot, row], psi[1, slot, row]], axis=1)
            value = jnp.dot(left, block, preferred_element_type=F32) * keep
            value = value.astype(BF)
            cols = value.shape[1] // 2
            applied.append(jnp.concatenate([value[:, :cols], value[:, cols:]], axis=0))
    total = None
    for g in range(4):
        rows = jnp.concatenate(applied[4 * g : 4 * g + 4], axis=1)
        right = r_refs[g][:, 0]
        right = right.reshape(right.shape[0] * right.shape[1], right.shape[2])
        term = jnp.dot(rows, right, preferred_element_type=F32)
        total = term if total is None else total + term
    out_ref[...] = total.reshape(out_ref.shape)


def compute(codes, pieces, lefts, rights):
    sec = codes.shape[2]
    v, _, _, dl, dr = pieces[0].shape
    any_spec = pl.BlockSpec(memory_space=pl.ANY)

    def env(x):
        return pl.BlockSpec((x.shape[0], 1) + x.shape[2:], lambda s, *_: (0, s, 0, 0))

    return pl.pallas_call(
        kernel,
        out_shape=jax.ShapeDtypeStruct((v, sec, dl, dr), F32),
        grid_spec=pltpu.PrefetchScalarGridSpec(
            num_scalar_prefetch=1,
            grid=(sec,),
            in_specs=[any_spec] * 7 + [env(x) for x in lefts + rights],
            out_specs=pl.BlockSpec((v, 1, dl, dr), lambda s, *_: (0, s, 0, 0)),
            scratch_shapes=[
                pltpu.VMEM((v, 16, sec, dl, dr), BF),
                pltpu.SemaphoreType.DMA((7,)),
            ],
        ),
        compiler_params=pltpu.CompilerParams(vmem_limit_bytes=32 * 2**20),
    )(codes, *pieces, *lefts, *rights)


def per_device(psi, left_env, right_env, source, active):
    sec_local = psi.shape[0]
    half = sec_local // 2
    m = lax.axis_index("mpo")
    sec = lax.axis_index("sec")

    def vector(v):
        return lax.dynamic_slice_in_dim(psi, v, 1, 1)[:, 0]

    own = jnp.stack([vector(m ^ 4), vector(m)])
    up = over_all(own, A_UP)
    down = over_all(own, A_DOWN)
    across = jnp.stack([over_all(up[0], A_UP), over_all(down[1], A_DOWN)])
    line = jnp.stack([own, up, down, across], axis=1)
    line_up = over_all(line, B_UP)
    line_down = over_all(line, B_DOWN)
    far0 = over_all(line_up[0, :2], B_UP)
    far1 = over_all(line_down[0, 2:], B_DOWN)
    near0 = over_all(line_up[1, :2], B_UP)
    near1 = over_all(line_down[1, 2:], B_DOWN)
    pieces = [line, line_up, line_down, far0, far1, near0, near1]

    rows = left_env.shape[2] // 2
    packed = jnp.concatenate([left_env[:, :, :rows], left_env[:, :, rows:]], axis=3)
    masked = jnp.where(active > 0, source, -1)

    def spread(x):
        mine = over_mpo(x, CORE)
        others = jnp.concatenate(
            [over_mpo(x[:, :half], X_DOWN), over_mpo(x[:, half:], X_UP)], axis=1
        )
        return [x, mine, others, over_mpo(others, CORE)]

    rights = spread(right_env)
    lefts = spread(packed)
    wanted = jnp.stack(spread(masked))

    group, row = wanted // sec_local, wanted % sec_local
    from_z = (group // SIDE - sec // SIDE) % SIDE
    from_y = (group % SIDE - sec % SIDE) % SIDE
    first = jnp.where(m % 2 == 0, from_z, from_y)
    second = jnp.where(m % 2 == 0, from_y, from_z)
    slot = slot_of(second) * SIDE + slot_of(first)
    codes = jnp.where(wanted >= 0, slot * sec_local + row, -1)

    partial = compute(codes, pieces, lefts, rights)
    arrived = over_mpo(partial[0].astype(BF), FAR)
    return (partial[1] + arrived.astype(F32)).astype(BF)[:, None]


def solution(mesh):
    placed = (
        P("sec", None, None, None),
        P("mpo", "sec", None, None),
        P("mpo", "sec", None, None),
        P("mpo", "sec"),
        P("mpo", "sec"),
    )
    return jax.shard_map(
        per_device,
        mesh=mesh,
        in_specs=placed,
        out_specs=P("sec", "mpo", None, None),
        check_vma=False,
    )
```

```python
import functools

import jax
import jax.numpy as jnp
from jax import lax
from jax.experimental import pallas as pl
from jax.experimental.pallas import tpu as pltpu
from jax.sharding import PartitionSpec as P

SIDE = 4
N_MPO = 8
BF = jnp.bfloat16
F32 = jnp.float32
PIECE, PIECES = 64, 4
PAIRS = 256
UNROLL = 16


def mpo_perm(fn):
    return [(m, fn(m)) for m in range(N_MPO)]


CORE = mpo_perm(lambda m: m ^ 1)
FAR = mpo_perm(lambda m: m ^ 4)
X_APART = mpo_perm(lambda m: (m - 2 + 4 * (m % 2)) % N_MPO)


def ring_perm(first, step):
    pairs = []
    for z in range(SIDE):
        for y in range(SIDE):
            for m in range(N_MPO):
                if (m % 2 == 0) == first:
                    to = ((z + step) % SIDE) * SIDE + y
                else:
                    to = z * SIDE + (y + step) % SIDE
                pairs.append(((z * SIDE + y) * N_MPO + m, to * N_MPO + m))
    return pairs


A_UP, A_DOWN, A_TWO = ring_perm(True, 1), ring_perm(True, -1), ring_perm(True, 2)
B_UP, B_DOWN = ring_perm(False, 1), ring_perm(False, -1)


def over_all(x, perm):
    return lax.ppermute(x, ("sec", "mpo"), perm)


def over_mpo(x, perm):
    return lax.ppermute(x, "mpo", perm)


def order(t):
    return jnp.where(t == 0, 0, jnp.where(t == 3, 1, jnp.where(t == 1, 2, 3)))


def list_kernel(place_ref, entry_ref, list_ref):
    def step(i, carry):
        list_ref[place_ref[i]] = entry_ref[i]
        return carry

    lax.fori_loop(0, place_ref.shape[0], step, 0, unroll=16)


def make_lists(codes):
    pair = lax.broadcasted_iota(jnp.int32, codes.shape, 0)
    row = jnp.where(codes >= 0, codes // PIECE, PIECES)
    rows = lax.broadcasted_iota(jnp.int32, (PIECES + 1, PAIRS), 0)
    chosen = (row[None] == rows).astype(jnp.int32)
    before = jnp.cumsum(chosen, axis=1) - chosen
    place = row * PAIRS + jnp.sum(before * chosen, axis=0)
    smem = pl.BlockSpec(memory_space=pltpu.SMEM)
    lists = pl.pallas_call(
        list_kernel,
        out_shape=jax.ShapeDtypeStruct(((PIECES + 1) * PAIRS,), jnp.int32),
        in_specs=[smem, smem],
        out_specs=smem,
    )(place, codes % PIECE * PAIRS + pair)
    return lists, jnp.sum(chosen, axis=1)


def term_kernel(lines, n_vec, n_env, fresh, list_ref, count_ref, *refs):
    envs, refs = refs[:n_env], refs[n_env:]
    psi_refs, refs = refs[: len(lines) * n_vec], refs[len(lines) * n_vec :]
    if not fresh:
        acc_refs, refs = refs[:n_vec], refs[n_vec:]
    out_refs, totals = refs[:n_vec], refs[n_vec:]
    sec, dl, dr = out_refs[0].shape

    for v in range(n_vec):
        if fresh:
            totals[v][...] = jnp.zeros_like(totals[v])
        else:
            totals[v][0:sec] = acc_refs[v][...]

    def rows_of(pair, first, last):
        value, start = None, 0
        for env in envs:
            size = env.shape[0]
            here = env[jnp.clip(pair - start, 0, size - 1), first:last, :]
            value = here if value is None else jnp.where(pair >= start, here, value)
            start += size
        return value

    def add(psis, line):
        count = count_ref[line]

        def step(i, carry):
            entries = []
            for u in range(UNROLL):
                there = i * UNROLL + u < count
                entry = jnp.where(there, list_ref[line * PAIRS + i * UNROLL + u], 0)
                pair = entry % PAIRS
                entries.append((entry // PAIRS, pair, jnp.where(there, pair % sec, sec)))
            values = []
            for at, pair, _ in entries:
                packed = rows_of(pair, dr, dr + dl // 2)
                left = jnp.concatenate([packed[:, :dl], packed[:, dl:]], axis=0)
                blocks = [psi[at] for psi in psis]
                block = blocks[0] if n_vec == 1 else jnp.concatenate(blocks, axis=1)
                value = jnp.dot(left, block, preferred_element_type=F32).astype(BF)
                if n_vec > 1:
                    value = jnp.concatenate(
                        [value[:, v * dr : (v + 1) * dr] for v in range(n_vec)], axis=0
                    )
                values.append(value)
            terms = []
            for value, (_, pair, _) in zip(values, entries):
                right = rows_of(pair, 0, dr)
                terms.append(jnp.dot(value, right, preferred_element_type=F32))
            for term, (_, _, to) in zip(terms, entries):
                for v in range(n_vec):
                    totals[v][to] += term[v * dl : (v + 1) * dl]
            return carry

        lax.fori_loop(0, (count + UNROLL - 1) // UNROLL, step, 0)

    for p, line in enumerate(lines):
        add(psi_refs[p * n_vec : (p + 1) * n_vec], line)
    for v in range(n_vec):
        out_refs[v][...] = totals[v][0:sec].astype(out_refs[v].dtype)


def add_terms(rows, lists, counts, envs, psis, accs, sec, dtype=F32):
    n_vec = len(psis[0])
    flat = [x for piece in psis for x in piece]
    _, dl, dr = flat[0].shape
    smem = pl.BlockSpec(memory_space=pltpu.SMEM)
    vmem = pl.BlockSpec(memory_space=pltpu.VMEM)
    return pl.pallas_call(
        functools.partial(term_kernel, rows, n_vec, len(envs), accs is None),
        out_shape=[jax.ShapeDtypeStruct((sec, dl, dr), dtype)] * n_vec,
        in_specs=[smem, smem] + [vmem] * (len(envs) + len(flat) + len(accs or [])),
        out_specs=[vmem] * n_vec,
        scratch_shapes=[pltpu.VMEM((sec + 1, dl, dr), F32)] * n_vec,
        compiler_params=pltpu.CompilerParams(vmem_limit_bytes=24 * 2**20),
        cost_estimate=pl.CostEstimate(
            flops=int(3e9), bytes_accessed=int(1.2e7), transcendentals=0
        ),
    )(lists, counts, *envs, *flat, *(accs or []))


def join_kernel(*refs):
    *arrays, out, sems = refs
    copies = []
    for k, ref in enumerate(arrays):
        size = ref.shape[0]
        copies.append(pltpu.make_async_copy(ref, out.at[k * size : (k + 1) * size], sems.at[k]))
    for copy in copies:
        copy.start()
    for copy in copies:
        copy.wait()


def join(arrays):
    first = arrays[0]
    return pl.pallas_call(
        join_kernel,
        out_shape=jax.ShapeDtypeStruct((first.shape[0] * len(arrays),) + first.shape[1:], first.dtype),
        in_specs=[pl.BlockSpec(memory_space=pl.ANY)] * len(arrays),
        out_specs=pl.BlockSpec(memory_space=pltpu.VMEM),
        scratch_shapes=[pltpu.SemaphoreType.DMA((len(arrays),))],
        compiler_params=pltpu.CompilerParams(vmem_limit_bytes=12 * 2**20),
        cost_estimate=pl.CostEstimate(flops=0, bytes_accessed=int(1e7), transcendentals=0),
    )(*arrays)


def copy_all(pairs, sems):
    copies = [pltpu.make_async_copy(x, y, sems.at[k]) for k, (x, y) in enumerate(pairs)]
    for copy in copies:
        copy.start()
    for copy in copies:
        copy.wait()


def start_kernel(psi, left, right, own, env, left_tile, sems):
    m = lax.axis_index("mpo")
    w_local, sec, dl, _ = left.shape
    dr = right.shape[3]
    rows = dl // 2
    takes = [pltpu.make_async_copy(psi.at[:, v], own.at[k], sems.at[k]) for k, v in enumerate((m ^ 4, m))]
    rights = [
        pltpu.make_async_copy(
            right.at[w], env.at[w * sec : (w + 1) * sec, 0:dr], sems.at[2 + w]
        )
        for w in range(w_local)
    ]
    load = pltpu.make_async_copy(left, left_tile, sems.at[2 + w_local])
    for copy in [*takes, load, *rights]:
        copy.start()
    load.wait()
    for w in range(w_local):
        tile = left_tile[w]
        env[w * sec : (w + 1) * sec, dr : dr + rows] = jnp.concatenate(
            [tile[:, :rows], tile[:, rows:]], axis=2
        )
    for copy in [*takes, *rights]:
        copy.wait()


def start(psi, left, right):
    w_local, sec, dl, _ = left.shape
    dr = right.shape[3]
    anywhere = pl.BlockSpec(memory_space=pltpu.HBM)
    return pl.pallas_call(
        start_kernel,
        out_shape=[
            jax.ShapeDtypeStruct((2, sec, dl, dr), BF),
            jax.ShapeDtypeStruct((w_local * sec, dr + dl // 2, dr), BF),
        ],
        in_specs=[anywhere] * 3,
        out_specs=[pl.BlockSpec(memory_space=pltpu.VMEM)] * 2,
        scratch_shapes=[
            pltpu.VMEM(left.shape, BF),
            pltpu.SemaphoreType.DMA((3 + w_local,)),
        ],
        compiler_params=pltpu.CompilerParams(vmem_limit_bytes=12 * 2**20),
        cost_estimate=pl.CostEstimate(flops=0, bytes_accessed=int(6e6), transcendentals=0),
    )(psi, left, right)


def line_kernel(*refs):
    *arrays, first, second, sems = refs
    size = arrays[0].shape[1]
    pairs = []
    for v, out in enumerate((first, second)):
        for k, x in enumerate(arrays):
            pairs.append((x.at[v], out.at[k * size : (k + 1) * size]))
    copy_all(pairs, sems)


def make_lines(arrays):
    _, size, dl, dr = arrays[0].shape
    out = jax.ShapeDtypeStruct((size * len(arrays), dl, dr), arrays[0].dtype)
    anywhere = pl.BlockSpec(memory_space=pl.ANY)
    return pl.pallas_call(
        line_kernel,
        out_shape=[out, out],
        in_specs=[anywhere] * len(arrays),
        out_specs=[pl.BlockSpec(memory_space=pltpu.VMEM)] * 2,
        scratch_shapes=[pltpu.SemaphoreType.DMA((2 * len(arrays),))],
        cost_estimate=pl.CostEstimate(flops=0, bytes_accessed=int(4e6), transcendentals=0),
    )(*arrays)


def per_device(psi, left_env, right_env, source, active):
    sec_local = psi.shape[0]
    m = lax.axis_index("mpo")
    sec = lax.axis_index("sec")
    dl, dr = psi.shape[2:]

    own, env = start(psi, left_env, right_env)
    up = over_all(own, A_UP)
    down = over_all(own, A_DOWN)
    across = over_all(own, A_TWO)

    env_core = over_mpo(env, CORE)
    masked = jnp.where(active > 0, source, -1)
    masked_apart = over_mpo(masked, X_APART)
    both = jnp.stack([masked, masked_apart])
    both_core = over_mpo(both, CORE)
    to_send, both = lax.optimization_barrier((env, both))
    env_apart = over_mpo(to_send, X_APART)

    across, env_core, both, both_core = lax.optimization_barrier((across, env_core, both, both_core))
    lines = make_lines([own, up, down, across])

    wanted = jnp.stack([both[0], both_core[0], both[1], both_core[1]])
    group, row = wanted // sec_local, wanted % sec_local
    from_z = (group // SIDE - sec // SIDE) % SIDE
    from_y = (group % SIDE - sec % SIDE) % SIDE
    first = jnp.where(m % 2 == 0, from_z, from_y)
    second = jnp.where(m % 2 == 0, from_y, from_z)
    slot = order(second) * SIDE + order(first)
    codes = jnp.where(wanted >= 0, slot * sec_local + row, -1)
    lists, counts = make_lists(codes.reshape(-1))

    lines_up = [over_all(line, B_UP) for line in lines]
    lines_down = [over_all(line, B_DOWN) for line in lines]
    lasts = [over_all(lines_up[0], B_UP), over_all(lines_down[1], B_DOWN)]
    env_apart, _, _, lists, counts = lax.optimization_barrier(
        (env_apart, lines_up[0], lines_down[1], lists, counts)
    )
    envs = [join([env, env_core]), env_apart, over_mpo(env_apart, CORE)]
    pieces = [[x[v] for x in (lines, lines_up, lines_down, lasts)] for v in range(2)]

    def added(v, rows, sums, kind=F32):
        return add_terms(rows, lists, counts, envs, [[pieces[v][k]] for k in rows], sums, sec_local, kind)

    (away,) = added(0, (2, 3), added(0, (0, 1), None), BF)
    arrived = over_mpo(away, FAR)
    (home,) = added(1, (1, 3), added(1, (0, 2), None))
    return (home + arrived.astype(F32)).astype(BF)[:, None]


def solution(mesh):
    placed = (
        P("sec", None, None, None),
        P("mpo", "sec", None, None),
        P("mpo", "sec", None, None),
        P("mpo", "sec"),
        P("mpo", "sec"),
    )
    return jax.shard_map(
        per_device,
        mesh=mesh,
        in_specs=placed,
        out_specs=P("sec", "mpo", None, None),
        check_vma=False,
    )
```

```python
import functools

import jax
import jax.numpy as jnp
from jax import lax
from jax.experimental import pallas as pl
from jax.experimental.pallas import tpu as pltpu
from jax.sharding import PartitionSpec as P

SIDE = 4
N_MPO = 8
BF = jnp.bfloat16
F32 = jnp.float32
PIECE, PIECES = 64, 4
PAIRS = 256
UNROLL = 16


def mpo_perm(fn):
    return [(m, fn(m)) for m in range(N_MPO)]


CORE = mpo_perm(lambda m: m ^ 1)
FAR = mpo_perm(lambda m: m ^ 4)
X_APART = mpo_perm(lambda m: (m - 2 + 4 * (m % 2)) % N_MPO)


def ring_perm(first, step):
    pairs = []
    for z in range(SIDE):
        for y in range(SIDE):
            for m in range(N_MPO):
                if (m % 2 == 0) == first:
                    to = ((z + step) % SIDE) * SIDE + y
                else:
                    to = z * SIDE + (y + step) % SIDE
                pairs.append(((z * SIDE + y) * N_MPO + m, to * N_MPO + m))
    return pairs


A_UP, A_DOWN, A_TWO = ring_perm(True, 1), ring_perm(True, -1), ring_perm(True, 2)
B_UP, B_DOWN = ring_perm(False, 1), ring_perm(False, -1)


def over_all(x, perm):
    return lax.ppermute(x, ("sec", "mpo"), perm)


def over_mpo(x, perm):
    return lax.ppermute(x, "mpo", perm)


def order(t):
    return jnp.where(t == 0, 0, jnp.where(t == 3, 1, jnp.where(t == 1, 2, 3)))


def list_kernel(place_ref, entry_ref, list_ref):
    def step(i, carry):
        list_ref[place_ref[i]] = entry_ref[i]
        return carry

    lax.fori_loop(0, place_ref.shape[0], step, 0, unroll=16)


def make_lists(codes):
    pair = lax.broadcasted_iota(jnp.int32, codes.shape, 0)
    row = jnp.where(codes >= 0, codes // PIECE, PIECES)
    rows = lax.broadcasted_iota(jnp.int32, (PIECES + 1, PAIRS), 0)
    chosen = (row[None] == rows).astype(jnp.int32)
    before = jnp.cumsum(chosen, axis=1) - chosen
    place = row * PAIRS + jnp.sum(before * chosen, axis=0)
    smem = pl.BlockSpec(memory_space=pltpu.SMEM)
    lists = pl.pallas_call(
        list_kernel,
        out_shape=jax.ShapeDtypeStruct(((PIECES + 1) * PAIRS,), jnp.int32),
        in_specs=[smem, smem],
        out_specs=smem,
    )(place, codes % PIECE * PAIRS + pair)
    return lists, jnp.sum(chosen, axis=1)


def term_kernel(lines, n_vec, n_env, fresh, list_ref, count_ref, *refs):
    envs, refs = refs[:n_env], refs[n_env:]
    psi_refs, refs = refs[: len(lines) * n_vec], refs[len(lines) * n_vec :]
    if not fresh:
        acc_refs, refs = refs[:n_vec], refs[n_vec:]
    out_refs, totals = refs[:n_vec], refs[n_vec:]
    sec, dl, dr = out_refs[0].shape

    for v in range(n_vec):
        if fresh:
            totals[v][...] = jnp.zeros_like(totals[v])
        else:
            totals[v][0:sec] = acc_refs[v][...]

    def rows_of(pair, first, last):
        value, start = None, 0
        for env in envs:
            size = env.shape[0]
            here = env[jnp.clip(pair - start, 0, size - 1), first:last, :]
            value = here if value is None else jnp.where(pair >= start, here, value)
            start += size
        return value

    def add(psis, line):
        count = count_ref[line]

        def step(i, carry):
            entries = []
            for u in range(UNROLL):
                there = i * UNROLL + u < count
                entry = jnp.where(there, list_ref[line * PAIRS + i * UNROLL + u], 0)
                pair = entry % PAIRS
                entries.append((entry // PAIRS, pair, jnp.where(there, pair % sec, sec)))
            values = []
            for at, pair, _ in entries:
                packed = rows_of(pair, dr, dr + dl // 2)
                left = jnp.concatenate([packed[:, :dl], packed[:, dl:]], axis=0)
                blocks = [psi[at] for psi in psis]
                block = blocks[0] if n_vec == 1 else jnp.concatenate(blocks, axis=1)
                value = jnp.dot(left, block, preferred_element_type=F32).astype(BF)
                if n_vec > 1:
                    value = jnp.concatenate(
                        [value[:, v * dr : (v + 1) * dr] for v in range(n_vec)], axis=0
                    )
                values.append(value)
            terms = []
            for value, (_, pair, _) in zip(values, entries):
                right = rows_of(pair, 0, dr)
                terms.append(jnp.dot(value, right, preferred_element_type=F32))
            for term, (_, _, to) in zip(terms, entries):
                for v in range(n_vec):
                    totals[v][to] += term[v * dl : (v + 1) * dl]
            return carry

        lax.fori_loop(0, (count + UNROLL - 1) // UNROLL, step, 0)

    for p, line in enumerate(lines):
        add(psi_refs[p * n_vec : (p + 1) * n_vec], line)
    for v in range(n_vec):
        out_refs[v][...] = totals[v][0:sec].astype(out_refs[v].dtype)


def add_terms(rows, lists, counts, envs, psis, accs, sec, dtype=F32):
    n_vec = len(psis[0])
    flat = [x for piece in psis for x in piece]
    _, dl, dr = flat[0].shape
    smem = pl.BlockSpec(memory_space=pltpu.SMEM)
    vmem = pl.BlockSpec(memory_space=pltpu.VMEM)
    return pl.pallas_call(
        functools.partial(term_kernel, rows, n_vec, len(envs), accs is None),
        out_shape=[jax.ShapeDtypeStruct((sec, dl, dr), dtype)] * n_vec,
        in_specs=[smem, smem] + [vmem] * (len(envs) + len(flat) + len(accs or [])),
        out_specs=[vmem] * n_vec,
        scratch_shapes=[pltpu.VMEM((sec + 1, dl, dr), F32)] * n_vec,
        compiler_params=pltpu.CompilerParams(vmem_limit_bytes=24 * 2**20),
        cost_estimate=pl.CostEstimate(
            flops=int(3e9), bytes_accessed=int(1.2e7), transcendentals=0
        ),
    )(lists, counts, *envs, *flat, *(accs or []))


def join_kernel(*refs):
    *arrays, out, sems = refs
    copies = []
    for k, ref in enumerate(arrays):
        size = ref.shape[0]
        copies.append(pltpu.make_async_copy(ref, out.at[k * size : (k + 1) * size], sems.at[k]))
    for copy in copies:
        copy.start()
    for copy in copies:
        copy.wait()


def join(arrays):
    first = arrays[0]
    return pl.pallas_call(
        join_kernel,
        out_shape=jax.ShapeDtypeStruct((first.shape[0] * len(arrays),) + first.shape[1:], first.dtype),
        in_specs=[pl.BlockSpec(memory_space=pl.ANY)] * len(arrays),
        out_specs=pl.BlockSpec(memory_space=pltpu.VMEM),
        scratch_shapes=[pltpu.SemaphoreType.DMA((len(arrays),))],
        compiler_params=pltpu.CompilerParams(vmem_limit_bytes=12 * 2**20),
        cost_estimate=pl.CostEstimate(flops=0, bytes_accessed=int(1e7), transcendentals=0),
    )(*arrays)


def line_kernel(*refs):
    *arrays, first, second = refs
    size = arrays[0].shape[1]
    for v, out in enumerate((first, second)):
        for k, x in enumerate(arrays):
            out[k * size : (k + 1) * size] = x[v]


def make_lines(arrays):
    _, size, dl, dr = arrays[0].shape
    blocks = size * len(arrays)
    vmem = pl.BlockSpec(memory_space=pltpu.VMEM)
    return pl.pallas_call(
        line_kernel,
        out_shape=[
            jax.ShapeDtypeStruct(shape, BF)
            for shape in ((blocks, dl, dr), (blocks, dl, dr))
        ],
        in_specs=[vmem] * len(arrays),
        out_specs=[vmem] * 2,
        compiler_params=pltpu.CompilerParams(vmem_limit_bytes=12 * 2**20),
        cost_estimate=pl.CostEstimate(flops=int(7e+09), bytes_accessed=int(4e6), transcendentals=0),
    )(*arrays)


def per_device(psi, left_env, right_env, source, active):
    sec_local = psi.shape[0]
    m = lax.axis_index("mpo")
    sec = lax.axis_index("sec")
    dl, dr = psi.shape[2:]

    own = jnp.stack([lax.dynamic_slice_in_dim(psi, v, 1, 1)[:, 0] for v in (m ^ 4, m)])
    up = over_all(own, A_UP)
    down = over_all(own, A_DOWN)
    across = over_all(own, A_TWO)

    rows = dl // 2
    packed = jnp.concatenate([left_env[:, :, :rows], left_env[:, :, rows:]], axis=3)
    env = jnp.concatenate([right_env, packed], axis=2).reshape(-1, dr + rows, dr)
    env_core = over_mpo(env, CORE)
    masked = jnp.where(active > 0, source, -1)
    masked_apart = over_mpo(masked, X_APART)
    both = jnp.stack([masked, masked_apart])
    both_core = over_mpo(both, CORE)
    to_send, both = lax.optimization_barrier((env, both))
    env_apart = over_mpo(to_send, X_APART)

    across, env_core, both, both_core = lax.optimization_barrier((across, env_core, both, both_core))
    lines = make_lines([own, up, down, across])

    wanted = jnp.stack([both[0], both_core[0], both[1], both_core[1]])
    group, row = wanted // sec_local, wanted % sec_local
    from_z = (group // SIDE - sec // SIDE) % SIDE
    from_y = (group % SIDE - sec % SIDE) % SIDE
    first = jnp.where(m % 2 == 0, from_z, from_y)
    second = jnp.where(m % 2 == 0, from_y, from_z)
    slot = order(second) * SIDE + order(first)
    codes = jnp.where(wanted >= 0, slot * sec_local + row, -1)
    lists, counts = make_lists(codes.reshape(-1))

    lines_up = [over_all(line, B_UP) for line in lines]
    lines_down = [over_all(line, B_DOWN) for line in lines]
    lasts = [over_all(lines_up[0], B_UP), over_all(lines_down[1], B_DOWN)]
    env_apart, _, _, lists, counts = lax.optimization_barrier(
        (env_apart, lines_up[0], lines_down[1], lists, counts)
    )
    envs = [join([env, env_core]), env_apart, over_mpo(env_apart, CORE)]
    pieces = [[x[v] for x in (lines, lines_up, lines_down, lasts)] for v in range(2)]

    def added(v, rows, sums, kind=F32):
        return add_terms(rows, lists, counts, envs, [[pieces[v][k]] for k in rows], sums, sec_local, kind)

    (away,) = added(0, (2, 3), added(0, (0, 1), None), BF)
    arrived = over_mpo(away, FAR)
    (home,) = added(1, (1, 3), added(1, (0, 2), None))
    return (home + arrived.astype(F32)).astype(BF)[:, None]


def solution(mesh):
    placed = (
        P("sec", None, None, None),
        P("mpo", "sec", None, None),
        P("mpo", "sec", None, None),
        P("mpo", "sec"),
        P("mpo", "sec"),
    )
    return jax.shard_map(
        per_device,
        mesh=mesh,
        in_specs=placed,
        out_specs=P("sec", "mpo", None, None),
        check_vma=False,
    )
```

```python
import functools

import jax
import jax.numpy as jnp
from jax import lax
from jax.experimental import pallas as pl
from jax.experimental.pallas import tpu as pltpu
from jax.sharding import PartitionSpec as P

SIDE = 4
N_MPO = 8
BF = jnp.bfloat16
F32 = jnp.float32
PIECE, PIECES = 64, 4
PAIRS = 256
UNROLL = 24


def mpo_perm(fn):
    return [(m, fn(m)) for m in range(N_MPO)]


CORE = mpo_perm(lambda m: m ^ 1)
FAR = mpo_perm(lambda m: m ^ 4)
X_APART = mpo_perm(lambda m: (m - 2 + 4 * (m % 2)) % N_MPO)


def ring_perm(first, step):
    pairs = []
    for z in range(SIDE):
        for y in range(SIDE):
            for m in range(N_MPO):
                if (m % 2 == 0) == first:
                    to = ((z + step) % SIDE) * SIDE + y
                else:
                    to = z * SIDE + (y + step) % SIDE
                pairs.append(((z * SIDE + y) * N_MPO + m, to * N_MPO + m))
    return pairs


A_UP, A_DOWN, A_TWO = ring_perm(True, 1), ring_perm(True, -1), ring_perm(True, 2)
B_UP, B_DOWN = ring_perm(False, 1), ring_perm(False, -1)


def over_all(x, perm):
    return lax.ppermute(x, ("sec", "mpo"), perm)


def over_mpo(x, perm):
    return lax.ppermute(x, "mpo", perm)


def order(t):
    return jnp.where(t == 0, 0, jnp.where(t == 3, 1, jnp.where(t == 1, 2, 3)))


def list_kernel(place_ref, entry_ref, list_ref):
    def step(i, carry):
        list_ref[place_ref[i]] = entry_ref[i]
        return carry

    lax.fori_loop(0, place_ref.shape[0], step, 0, unroll=16)


def make_lists(codes):
    pair = lax.broadcasted_iota(jnp.int32, codes.shape, 0)
    row = jnp.where(codes >= 0, codes // PIECE, PIECES)
    rows = lax.broadcasted_iota(jnp.int32, (PIECES + 1, PAIRS), 0)
    chosen = (row[None] == rows).astype(jnp.int32)
    before = jnp.cumsum(chosen, axis=1) - chosen
    place = row * PAIRS + jnp.sum(before * chosen, axis=0)
    smem = pl.BlockSpec(memory_space=pltpu.SMEM)
    lists = pl.pallas_call(
        list_kernel,
        out_shape=jax.ShapeDtypeStruct(((PIECES + 1) * PAIRS,), jnp.int32),
        in_specs=[smem, smem],
        out_specs=smem,
    )(place, codes % PIECE * PAIRS + pair)
    return lists, jnp.sum(chosen, axis=1)


def term_kernel(plan, n_vec, n_env, fresh, list_ref, count_ref, *refs):
    envs, refs = refs[:n_env], list(refs[n_env:])
    psis = [[refs.pop(0) for _ in vectors] for _, vectors in plan]
    if not fresh:
        acc_refs, refs = refs[:n_vec], refs[n_vec:]
    out_refs, totals = refs[:n_vec], refs[n_vec:]
    sec, dl, dr = out_refs[0].shape

    for v in range(n_vec):
        if fresh:
            totals[v][...] = jnp.zeros_like(totals[v])
        else:
            totals[v][0:sec] = acc_refs[v][...]

    def rows_of(pair, first, last):
        value, start = None, 0
        for env in envs:
            size = env.shape[0]
            here = env[jnp.clip(pair - start, 0, size - 1), first:last, :]
            value = here if value is None else jnp.where(pair >= start, here, value)
            start += size
        return value

    def add(psis, vectors, line):
        count = count_ref[line]

        def step(i, carry):
            entries = []
            for u in range(UNROLL):
                there = i * UNROLL + u < count
                entry = jnp.where(there, list_ref[line * PAIRS + i * UNROLL + u], 0)
                pair = entry % PAIRS
                entries.append((entry // PAIRS, pair, jnp.where(there, pair % sec, sec)))
            values = []
            for at, pair, _ in entries:
                packed = rows_of(pair, dr, dr + dl // 2)
                left = jnp.concatenate([packed[:, :dl], packed[:, dl:]], axis=0)
                blocks = [psi[at] for psi in psis]
                block = blocks[0] if len(psis) == 1 else jnp.concatenate(blocks, axis=1)
                value = jnp.dot(left, block, preferred_element_type=F32).astype(BF)
                if len(psis) > 1:
                    parts = [value[:, k * dr : (k + 1) * dr] for k in range(len(psis))]
                    value = jnp.concatenate(parts, axis=0)
                values.append(value)
            terms = []
            for value, (_, pair, _) in zip(values, entries):
                right = rows_of(pair, 0, dr)
                terms.append(jnp.dot(value, right, preferred_element_type=F32))
            for term, (_, _, to) in zip(terms, entries):
                for k, v in enumerate(vectors):
                    totals[v][to] += term[k * dl : (k + 1) * dl]
            return carry

        lax.fori_loop(0, (count + UNROLL - 1) // UNROLL, step, 0)

    for arrays, (line, vectors) in zip(psis, plan):
        add(arrays, vectors, line)
    for v in range(n_vec):
        out_refs[v][...] = totals[v][0:sec].astype(out_refs[v].dtype)


def add_terms(plan, lists, counts, envs, psis, accs, n_vec, sec, dtype=F32):
    dl, dr = psis[0].shape[1:]
    smem = pl.BlockSpec(memory_space=pltpu.SMEM)
    vmem = pl.BlockSpec(memory_space=pltpu.VMEM)
    return pl.pallas_call(
        functools.partial(term_kernel, plan, n_vec, len(envs), accs is None),
        out_shape=[jax.ShapeDtypeStruct((sec, dl, dr), dtype)] * n_vec,
        in_specs=[smem, smem] + [vmem] * (len(envs) + len(psis) + len(accs or [])),
        out_specs=[vmem] * n_vec,
        scratch_shapes=[pltpu.VMEM((sec + 1, dl, dr), F32)] * n_vec,
        compiler_params=pltpu.CompilerParams(vmem_limit_bytes=24 * 2**20),
        cost_estimate=pl.CostEstimate(
            flops=int(3e9), bytes_accessed=int(1.2e7), transcendentals=0
        ),
    )(lists, counts, *envs, *psis, *(accs or []))


def join_kernel(*refs):
    *arrays, out, sems = refs
    copies = []
    for k, ref in enumerate(arrays):
        size = ref.shape[0]
        copies.append(pltpu.make_async_copy(ref, out.at[k * size : (k + 1) * size], sems.at[k]))
    for copy in copies:
        copy.start()
    for copy in copies:
        copy.wait()


def join(arrays):
    first = arrays[0]
    return pl.pallas_call(
        join_kernel,
        out_shape=jax.ShapeDtypeStruct((first.shape[0] * len(arrays),) + first.shape[1:], first.dtype),
        in_specs=[pl.BlockSpec(memory_space=pl.ANY)] * len(arrays),
        out_specs=pl.BlockSpec(memory_space=pltpu.VMEM),
        scratch_shapes=[pltpu.SemaphoreType.DMA((len(arrays),))],
        compiler_params=pltpu.CompilerParams(vmem_limit_bytes=16 * 2**20),
        cost_estimate=pl.CostEstimate(flops=0, bytes_accessed=int(1e7), transcendentals=0),
    )(*arrays)


def line_kernel(*refs):
    *arrays, first, second = refs
    size = arrays[0].shape[1]
    for v, out in enumerate((first, second)):
        for k, x in enumerate(arrays):
            out[k * size : (k + 1) * size] = x[v]


def make_lines(arrays):
    _, size, dl, dr = arrays[0].shape
    blocks = size * len(arrays)
    vmem = pl.BlockSpec(memory_space=pltpu.VMEM)
    return pl.pallas_call(
        line_kernel,
        out_shape=[
            jax.ShapeDtypeStruct(shape, BF)
            for shape in ((blocks, dl, dr), (blocks, dl, dr))
        ],
        in_specs=[vmem] * len(arrays),
        out_specs=[vmem] * 2,
        compiler_params=pltpu.CompilerParams(vmem_limit_bytes=12 * 2**20),
        cost_estimate=pl.CostEstimate(flops=int(7e+09), bytes_accessed=int(4e6), transcendentals=0),
    )(*arrays)


def per_device(psi, left_env, right_env, source, active):
    sec_local = psi.shape[0]
    m = lax.axis_index("mpo")
    sec = lax.axis_index("sec")
    dl, dr = psi.shape[2:]

    own = jnp.stack([lax.dynamic_slice_in_dim(psi, v, 1, 1)[:, 0] for v in (m ^ 4, m)])
    up = over_all(own, A_UP)
    down = over_all(own, A_DOWN)
    across = over_all(own, A_TWO)

    rows = dl // 2
    packed = jnp.concatenate([left_env[:, :, :rows], left_env[:, :, rows:]], axis=3)
    env = jnp.concatenate([right_env, packed], axis=2).reshape(-1, dr + rows, dr)
    env_core = over_mpo(env, CORE)
    masked = jnp.where(active > 0, source, -1)
    masked_apart = over_mpo(masked, X_APART)
    both = jnp.stack([masked, masked_apart])
    both_core = over_mpo(both, CORE)
    to_send, both = lax.optimization_barrier((env, both))
    env_apart = over_mpo(to_send, X_APART)

    across, env_core, both, both_core = lax.optimization_barrier((across, env_core, both, both_core))
    lines = make_lines([own, up, down, across])

    wanted = jnp.stack([both[0], both_core[0], both[1], both_core[1]])
    group, row = wanted // sec_local, wanted % sec_local
    from_z = (group // SIDE - sec // SIDE) % SIDE
    from_y = (group % SIDE - sec % SIDE) % SIDE
    first = jnp.where(m % 2 == 0, from_z, from_y)
    second = jnp.where(m % 2 == 0, from_y, from_z)
    slot = order(second) * SIDE + order(first)
    codes = jnp.where(wanted >= 0, slot * sec_local + row, -1)
    lists, counts = make_lists(codes.reshape(-1))

    lines_up = [over_all(line, B_UP) for line in lines]
    lines_down = [over_all(line, B_DOWN) for line in lines]
    lasts = [over_all(lines_up[0], B_UP), over_all(lines_down[1], B_DOWN)]
    env_apart, _, _, lists, counts = lax.optimization_barrier(
        (env_apart, lines_up[0], lines_down[1], lists, counts)
    )
    envs = [join([env, env_core, env_apart, over_mpo(env_apart, CORE)])]

    def added(plan, psis, sums, kind=F32):
        n_vec = 1 if sums else 2
        return add_terms(plan, lists, counts, envs, psis, sums, n_vec, sec_local, kind)

    plan = [(0, (0, 1)), (1, (0,))]
    away, home = added(plan, [lines[0], lines[1], lines_up[0]], None)
    (away,) = added([(2, (0,)), (3, (0,))], [lines_down[0], lasts[0]], [away], BF)
    arrived = over_mpo(away, FAR)
    (home,) = added([(2, (0,))], [lines_down[1]], [home])
    (home,) = added([(1, (0,)), (3, (0,))], [lines_up[1], lasts[1]], [home])
    return (home + arrived.astype(F32)).astype(BF)[:, None]


def solution(mesh):
    placed = (
        P("sec", None, None, None),
        P("mpo", "sec", None, None),
        P("mpo", "sec", None, None),
        P("mpo", "sec"),
        P("mpo", "sec"),
    )
    return jax.shard_map(
        per_device,
        mesh=mesh,
        in_specs=placed,
        out_specs=P("sec", "mpo", None, None),
        check_vma=False,
    )
```

```python
import functools

import jax
import jax.numpy as jnp
from jax import lax
from jax.experimental import pallas as pl
from jax.experimental.pallas import tpu as pltpu
from jax.sharding import PartitionSpec as P

SIDE = 4
N_MPO = 8
BF = jnp.bfloat16
F32 = jnp.float32
PIECE, PIECES = 64, 4
PAIRS = 256
UNROLL = 24


def mpo_perm(fn):
    return [(m, fn(m)) for m in range(N_MPO)]


CORE = mpo_perm(lambda m: m ^ 1)
FAR = mpo_perm(lambda m: m ^ 4)
X_APART = mpo_perm(lambda m: (m - 2 + 4 * (m % 2)) % N_MPO)


def ring_perm(first, step):
    pairs = []
    for z in range(SIDE):
        for y in range(SIDE):
            for m in range(N_MPO):
                if (m % 2 == 0) == first:
                    to = ((z + step) % SIDE) * SIDE + y
                else:
                    to = z * SIDE + (y + step) % SIDE
                pairs.append(((z * SIDE + y) * N_MPO + m, to * N_MPO + m))
    return pairs


A_UP, A_DOWN, A_TWO = ring_perm(True, 1), ring_perm(True, -1), ring_perm(True, 2)
B_UP, B_DOWN = ring_perm(False, 1), ring_perm(False, -1)


def over_all(x, perm):
    return lax.ppermute(x, ("sec", "mpo"), perm)


def over_mpo(x, perm):
    return lax.ppermute(x, "mpo", perm)


def order(t):
    return jnp.where(t == 0, 0, jnp.where(t == 3, 1, jnp.where(t == 1, 2, 3)))


def list_kernel(place_ref, entry_ref, list_ref):
    def step(i, carry):
        list_ref[place_ref[i]] = entry_ref[i]
        return carry

    lax.fori_loop(0, place_ref.shape[0], step, 0, unroll=16)


def make_lists(codes):
    pair = lax.broadcasted_iota(jnp.int32, codes.shape, 0)
    row = jnp.where(codes >= 0, codes // PIECE, PIECES)
    rows = lax.broadcasted_iota(jnp.int32, (PIECES + 1, PAIRS), 0)
    chosen = (row[None] == rows).astype(jnp.int32)
    before = jnp.cumsum(chosen, axis=1) - chosen
    place = row * PAIRS + jnp.sum(before * chosen, axis=0)
    smem = pl.BlockSpec(memory_space=pltpu.SMEM)
    lists = pl.pallas_call(
        list_kernel,
        out_shape=jax.ShapeDtypeStruct(((PIECES + 1) * PAIRS,), jnp.int32),
        in_specs=[smem, smem],
        out_specs=smem,
    )(place, codes % PIECE * PAIRS + pair)
    return lists, jnp.sum(chosen, axis=1)


def term_kernel(plan, n_vec, n_env, fresh, list_ref, count_ref, *refs):
    envs, refs = refs[:n_env], list(refs[n_env:])
    psis = [[refs.pop(0) for _ in vectors] for _, vectors in plan]
    if not fresh:
        acc_refs, refs = refs[:n_vec], refs[n_vec:]
    out_refs, totals = refs[:n_vec], refs[n_vec:]
    sec, dl, dr = out_refs[0].shape

    for v in range(n_vec):
        if fresh:
            totals[v][...] = jnp.zeros_like(totals[v])
        else:
            totals[v][0:sec] = acc_refs[v][...]

    def rows_of(pair, first, last):
        value, start = None, 0
        for env in envs:
            size = env.shape[0]
            here = env[jnp.clip(pair - start, 0, size - 1), first:last, :]
            value = here if value is None else jnp.where(pair >= start, here, value)
            start += size
        return value

    def add(psis, vectors, line):
        count = count_ref[line]

        def step(i, carry):
            entries = []
            for u in range(UNROLL):
                there = i * UNROLL + u < count
                entry = jnp.where(there, list_ref[line * PAIRS + i * UNROLL + u], 0)
                pair = entry % PAIRS
                entries.append((entry // PAIRS, pair, jnp.where(there, pair % sec, sec)))
            values = []
            for at, pair, _ in entries:
                packed = rows_of(pair, dr, dr + dl // 2)
                left = jnp.concatenate([packed[:, :dl], packed[:, dl:]], axis=0)
                blocks = [psi[at] for psi in psis]
                block = blocks[0] if len(psis) == 1 else jnp.concatenate(blocks, axis=1)
                value = jnp.dot(left, block, preferred_element_type=F32).astype(BF)
                if len(psis) > 1:
                    parts = [value[:, k * dr : (k + 1) * dr] for k in range(len(psis))]
                    value = jnp.concatenate(parts, axis=0)
                values.append(value)
            terms = []
            for value, (_, pair, _) in zip(values, entries):
                right = rows_of(pair, 0, dr)
                terms.append(jnp.dot(value, right, preferred_element_type=F32))
            for term, (_, _, to) in zip(terms, entries):
                for k, v in enumerate(vectors):
                    totals[v][to] += term[k * dl : (k + 1) * dl]
            return carry

        lax.fori_loop(0, (count + UNROLL - 1) // UNROLL, step, 0)

    for arrays, (line, vectors) in zip(psis, plan):
        add(arrays, vectors, line)
    for v in range(n_vec):
        out_refs[v][...] = totals[v][0:sec].astype(out_refs[v].dtype)


def add_terms(plan, lists, counts, envs, psis, accs, n_vec, sec, dtype=F32):
    dl, dr = psis[0].shape[1:]
    smem = pl.BlockSpec(memory_space=pltpu.SMEM)
    vmem = pl.BlockSpec(memory_space=pltpu.VMEM)
    return pl.pallas_call(
        functools.partial(term_kernel, plan, n_vec, len(envs), accs is None),
        out_shape=[jax.ShapeDtypeStruct((sec, dl, dr), dtype)] * n_vec,
        in_specs=[smem, smem] + [vmem] * (len(envs) + len(psis) + len(accs or [])),
        out_specs=[vmem] * n_vec,
        scratch_shapes=[pltpu.VMEM((sec + 1, dl, dr), F32)] * n_vec,
        compiler_params=pltpu.CompilerParams(vmem_limit_bytes=24 * 2**20),
        cost_estimate=pl.CostEstimate(
            flops=int(3e9), bytes_accessed=int(1.2e7), transcendentals=0
        ),
    )(lists, counts, *envs, *psis, *(accs or []))


def join_kernel(*refs):
    *arrays, out, sems = refs
    copies = []
    for k, ref in enumerate(arrays):
        size = ref.shape[0]
        copies.append(pltpu.make_async_copy(ref, out.at[k * size : (k + 1) * size], sems.at[k]))
    for copy in copies:
        copy.start()
    for copy in copies:
        copy.wait()


def join(arrays):
    first = arrays[0]
    return pl.pallas_call(
        join_kernel,
        out_shape=jax.ShapeDtypeStruct((first.shape[0] * len(arrays),) + first.shape[1:], first.dtype),
        in_specs=[pl.BlockSpec(memory_space=pl.ANY)] * len(arrays),
        out_specs=pl.BlockSpec(memory_space=pltpu.VMEM),
        scratch_shapes=[pltpu.SemaphoreType.DMA((len(arrays),))],
        compiler_params=pltpu.CompilerParams(vmem_limit_bytes=16 * 2**20),
        cost_estimate=pl.CostEstimate(flops=0, bytes_accessed=int(1e7), transcendentals=0),
    )(*arrays)


def line_kernel(*refs):
    *arrays, first, second = refs
    size = arrays[0].shape[1]
    for v, out in enumerate((first, second)):
        for k, x in enumerate(arrays):
            out[k * size : (k + 1) * size] = x[v]


def make_lines(arrays):
    _, size, dl, dr = arrays[0].shape
    blocks = size * len(arrays)
    vmem = pl.BlockSpec(memory_space=pltpu.VMEM)
    return pl.pallas_call(
        line_kernel,
        out_shape=[
            jax.ShapeDtypeStruct(shape, BF)
            for shape in ((blocks, dl, dr), (blocks, dl, dr))
        ],
        in_specs=[vmem] * len(arrays),
        out_specs=[vmem] * 2,
        compiler_params=pltpu.CompilerParams(vmem_limit_bytes=12 * 2**20),
        cost_estimate=pl.CostEstimate(flops=int(7e+09), bytes_accessed=int(4e6), transcendentals=0),
    )(*arrays)


def per_device(psi, left_env, right_env, source, active):
    sec_local = psi.shape[0]
    m = lax.axis_index("mpo")
    sec = lax.axis_index("sec")
    dl, dr = psi.shape[2:]

    own = jnp.stack([lax.dynamic_slice_in_dim(psi, v, 1, 1)[:, 0] for v in (m ^ 4, m)])
    up = over_all(own, A_UP)
    down = over_all(own, A_DOWN)
    across = over_all(own, A_TWO)

    rows = dl // 2
    packed = jnp.concatenate([left_env[:, :, :rows], left_env[:, :, rows:]], axis=3)
    env = jnp.concatenate([right_env, packed], axis=2).reshape(-1, dr + rows, dr)
    env_core = over_mpo(env, CORE)
    masked = jnp.where(active > 0, source, -1)
    masked_apart = over_mpo(masked, X_APART)
    both = jnp.stack([masked, masked_apart])
    both_core = over_mpo(both, CORE)
    to_send, both = lax.optimization_barrier((env, both))
    env_apart = over_mpo(to_send, X_APART)

    across, env_core, both, both_core = lax.optimization_barrier((across, env_core, both, both_core))
    lines = make_lines([own, up, down, across])

    wanted = jnp.stack([both[0], both_core[0], both[1], both_core[1]])
    group, row = wanted // sec_local, wanted % sec_local
    from_z = (group // SIDE - sec // SIDE) % SIDE
    from_y = (group % SIDE - sec % SIDE) % SIDE
    first = jnp.where(m % 2 == 0, from_z, from_y)
    second = jnp.where(m % 2 == 0, from_y, from_z)
    slot = order(second) * SIDE + order(first)
    codes = jnp.where(wanted >= 0, slot * sec_local + row, -1)
    lists, counts = make_lists(codes.reshape(-1))

    lines_up = [over_all(line, B_UP) for line in lines]
    lines_down = [over_all(line, B_DOWN) for line in lines]
    lasts = [over_all(lines_up[0], B_UP), over_all(lines_down[1], B_DOWN)]
    env_apart, _, _, lists, counts = lax.optimization_barrier(
        (env_apart, lines_up[0], lines_down[1], lists, counts)
    )
    envs = [join([env, env_core, env_apart, over_mpo(env_apart, CORE)])]

    def added(plan, psis, sums, kind=F32):
        n_vec = 1 if sums else 2
        return add_terms(plan, lists, counts, envs, psis, sums, n_vec, sec_local, kind)

    plan = [(0, (0, 1)), (1, (0,))]
    away, home = added(plan, [lines[0], lines[1], lines_up[0]], None)
    (away,) = added([(3, (0,))], [lasts[0]], [away])
    (away,) = added([(2, (0,))], [lines_down[0]], [away], BF)
    arrived = over_mpo(away, FAR)
    (home,) = added([(2, (0,))], [lines_down[1]], [home])
    (home,) = added([(1, (0,)), (3, (0,))], [lines_up[1], lasts[1]], [home])
    return (home + arrived.astype(F32)).astype(BF)[:, None]


def solution(mesh):
    placed = (
        P("sec", None, None, None),
        P("mpo", "sec", None, None),
        P("mpo", "sec", None, None),
        P("mpo", "sec"),
        P("mpo", "sec"),
    )
    return jax.shard_map(
        per_device,
        mesh=mesh,
        in_specs=placed,
        out_specs=P("sec", "mpo", None, None),
        check_vma=False,
    )
```

```python
import functools

import jax
import jax.numpy as jnp
from jax import lax
from jax.experimental import pallas as pl
from jax.experimental.pallas import tpu as pltpu
from jax.sharding import PartitionSpec as P

SIDE = 4
N_MPO = 8
BF = jnp.bfloat16
F32 = jnp.float32
PIECE, PIECES = 64, 4
PAIRS = 256
UNROLL = 24


def mpo_perm(fn):
    return [(m, fn(m)) for m in range(N_MPO)]


CORE = mpo_perm(lambda m: m ^ 1)
FAR = mpo_perm(lambda m: m ^ 4)
X_APART = mpo_perm(lambda m: (m - 2 + 4 * (m % 2)) % N_MPO)


def ring_perm(first, step):
    pairs = []
    for z in range(SIDE):
        for y in range(SIDE):
            for m in range(N_MPO):
                if (m % 2 == 0) == first:
                    to = ((z + step) % SIDE) * SIDE + y
                else:
                    to = z * SIDE + (y + step) % SIDE
                pairs.append(((z * SIDE + y) * N_MPO + m, to * N_MPO + m))
    return pairs


A_UP, A_DOWN, A_TWO = ring_perm(True, 1), ring_perm(True, -1), ring_perm(True, 2)
B_UP, B_DOWN = ring_perm(False, 1), ring_perm(False, -1)


def over_all(x, perm):
    return lax.ppermute(x, ("sec", "mpo"), perm)


def over_mpo(x, perm):
    return lax.ppermute(x, "mpo", perm)


def order(t):
    return jnp.where(t == 0, 0, jnp.where(t == 3, 1, jnp.where(t == 1, 2, 3)))


def list_kernel(place_ref, entry_ref, list_ref):
    def step(i, carry):
        list_ref[place_ref[i]] = entry_ref[i]
        return carry

    lax.fori_loop(0, place_ref.shape[0], step, 0, unroll=16)


def make_lists(codes):
    pair = lax.broadcasted_iota(jnp.int32, codes.shape, 0)
    row = jnp.where(codes >= 0, codes // PIECE, PIECES)
    rows = lax.broadcasted_iota(jnp.int32, (PIECES + 1, PAIRS), 0)
    chosen = (row[None] == rows).astype(jnp.int32)
    before = jnp.cumsum(chosen, axis=1) - chosen
    place = row * PAIRS + jnp.sum(before * chosen, axis=0)
    smem = pl.BlockSpec(memory_space=pltpu.SMEM)
    lists = pl.pallas_call(
        list_kernel,
        out_shape=jax.ShapeDtypeStruct(((PIECES + 1) * PAIRS,), jnp.int32),
        in_specs=[smem, smem],
        out_specs=smem,
    )(place, codes % PIECE * PAIRS + pair)
    return lists, jnp.sum(chosen, axis=1)


def term_kernel(plan, n_vec, n_env, fresh, list_ref, count_ref, *refs):
    envs, refs = refs[:n_env], list(refs[n_env:])
    psis = [[refs.pop(0) for _ in vectors] for _, vectors in plan]
    if not fresh:
        acc_refs, refs = refs[:n_vec], refs[n_vec:]
    out_refs, totals = refs[:n_vec], refs[n_vec:]
    sec, dl, dr = out_refs[0].shape

    for v in range(n_vec):
        if fresh:
            totals[v][...] = jnp.zeros_like(totals[v])
        else:
            totals[v][0:sec] = acc_refs[v][...]

    def rows_of(pair, first, last):
        value, start = None, 0
        for env in envs:
            size = env.shape[0]
            here = env[jnp.clip(pair - start, 0, size - 1), first:last, :]
            value = here if value is None else jnp.where(pair >= start, here, value)
            start += size
        return value

    def add(psis, vectors, line):
        count = count_ref[line]

        def step(i, carry):
            entries = []
            for u in range(UNROLL):
                there = i * UNROLL + u < count
                entry = jnp.where(there, list_ref[line * PAIRS + i * UNROLL + u], 0)
                pair = entry % PAIRS
                entries.append((entry // PAIRS, pair, jnp.where(there, pair % sec, sec)))
            values = []
            for at, pair, _ in entries:
                packed = rows_of(pair, dr, dr + dl // 2)
                left = jnp.concatenate([packed[:, :dl], packed[:, dl:]], axis=0)
                blocks = [psi[at] for psi in psis]
                block = blocks[0] if len(psis) == 1 else jnp.concatenate(blocks, axis=1)
                value = jnp.dot(left, block, preferred_element_type=F32).astype(BF)
                if len(psis) > 1:
                    parts = [value[:, k * dr : (k + 1) * dr] for k in range(len(psis))]
                    value = jnp.concatenate(parts, axis=0)
                values.append(value)
            terms = []
            for value, (_, pair, _) in zip(values, entries):
                right = rows_of(pair, 0, dr)
                terms.append(jnp.dot(value, right, preferred_element_type=F32))
            for term, (_, _, to) in zip(terms, entries):
                for k, v in enumerate(vectors):
                    totals[v][to] += term[k * dl : (k + 1) * dl]
            return carry

        lax.fori_loop(0, (count + UNROLL - 1) // UNROLL, step, 0)

    for arrays, (line, vectors) in zip(psis, plan):
        add(arrays, vectors, line)
    for v in range(n_vec):
        out_refs[v][...] = totals[v][0:sec].astype(out_refs[v].dtype)


def add_terms(plan, lists, counts, envs, psis, accs, n_vec, sec, dtype=F32):
    dl, dr = psis[0].shape[1:]
    smem = pl.BlockSpec(memory_space=pltpu.SMEM)
    vmem = pl.BlockSpec(memory_space=pltpu.VMEM)
    return pl.pallas_call(
        functools.partial(term_kernel, plan, n_vec, len(envs), accs is None),
        out_shape=[jax.ShapeDtypeStruct((sec, dl, dr), dtype)] * n_vec,
        in_specs=[smem, smem] + [vmem] * (len(envs) + len(psis) + len(accs or [])),
        out_specs=[vmem] * n_vec,
        scratch_shapes=[pltpu.VMEM((sec + 1, dl, dr), F32)] * n_vec,
        compiler_params=pltpu.CompilerParams(vmem_limit_bytes=24 * 2**20),
        cost_estimate=pl.CostEstimate(
            flops=int(3e9), bytes_accessed=int(1.2e7), transcendentals=0
        ),
    )(lists, counts, *envs, *psis, *(accs or []))


def join_kernel(*refs):
    *arrays, out, sems = refs
    copies = []
    for k, ref in enumerate(arrays):
        size = ref.shape[0]
        copies.append(pltpu.make_async_copy(ref, out.at[k * size : (k + 1) * size], sems.at[k]))
    for copy in copies:
        copy.start()
    for copy in copies:
        copy.wait()


def join(arrays):
    first = arrays[0]
    return pl.pallas_call(
        join_kernel,
        out_shape=jax.ShapeDtypeStruct((first.shape[0] * len(arrays),) + first.shape[1:], first.dtype),
        in_specs=[pl.BlockSpec(memory_space=pl.ANY)] * len(arrays),
        out_specs=pl.BlockSpec(memory_space=pltpu.VMEM),
        scratch_shapes=[pltpu.SemaphoreType.DMA((len(arrays),))],
        compiler_params=pltpu.CompilerParams(vmem_limit_bytes=16 * 2**20),
        cost_estimate=pl.CostEstimate(flops=0, bytes_accessed=int(1e7), transcendentals=0),
    )(*arrays)


def line_kernel(*refs):
    *arrays, first, second = refs
    size = arrays[0].shape[1]
    for v, out in enumerate((first, second)):
        for k, x in enumerate(arrays):
            out[k * size : (k + 1) * size] = x[v]


def make_lines(arrays):
    _, size, dl, dr = arrays[0].shape
    blocks = size * len(arrays)
    vmem = pl.BlockSpec(memory_space=pltpu.VMEM)
    return pl.pallas_call(
        line_kernel,
        out_shape=[
            jax.ShapeDtypeStruct(shape, BF)
            for shape in ((blocks, dl, dr), (blocks, dl, dr))
        ],
        in_specs=[vmem] * len(arrays),
        out_specs=[vmem] * 2,
        compiler_params=pltpu.CompilerParams(vmem_limit_bytes=12 * 2**20),
        cost_estimate=pl.CostEstimate(flops=int(7e+09), bytes_accessed=int(4e6), transcendentals=0),
    )(*arrays)


def per_device(psi, left_env, right_env, source, active):
    sec_local = psi.shape[0]
    m = lax.axis_index("mpo")
    sec = lax.axis_index("sec")
    dl, dr = psi.shape[2:]

    own = jnp.stack([lax.dynamic_slice_in_dim(psi, v, 1, 1)[:, 0] for v in (m ^ 4, m)])
    up = over_all(own, A_UP)
    down = over_all(own, A_DOWN)
    across = over_all(own, A_TWO)

    rows = dl // 2
    packed = jnp.concatenate([left_env[:, :, :rows], left_env[:, :, rows:]], axis=3)
    env = jnp.concatenate([right_env, packed], axis=2).reshape(-1, dr + rows, dr)
    env_core = over_mpo(env, CORE)
    masked = jnp.where(active > 0, source, -1)
    masked_apart = over_mpo(masked, X_APART)
    both = jnp.stack([masked, masked_apart])
    both_core = over_mpo(both, CORE)
    to_send, both = lax.optimization_barrier((env, both))
    env_apart = over_mpo(to_send, X_APART)

    across, both, both_core = lax.optimization_barrier((across, both, both_core))
    lines = make_lines([own, up, down, across])

    wanted = jnp.stack([both[0], both_core[0], both[1], both_core[1]])
    group, row = wanted // sec_local, wanted % sec_local
    from_z = (group // SIDE - sec // SIDE) % SIDE
    from_y = (group % SIDE - sec % SIDE) % SIDE
    first = jnp.where(m % 2 == 0, from_z, from_y)
    second = jnp.where(m % 2 == 0, from_y, from_z)
    slot = order(second) * SIDE + order(first)
    codes = jnp.where(wanted >= 0, slot * sec_local + row, -1)
    lists, counts = make_lists(codes.reshape(-1))

    lines_up = [over_all(line, B_UP) for line in lines]
    lines_down = [over_all(line, B_DOWN) for line in lines]
    lasts = [over_all(lines_up[0], B_UP), over_all(lines_down[1], B_DOWN)]
    env_apart, _, _, lists, counts = lax.optimization_barrier(
        (env_apart, lines_up[0], lines_down[1], lists, counts)
    )
    envs = [join([env, env_core, env_apart, over_mpo(env_apart, CORE)])]

    def added(plan, psis, sums, kind=F32):
        n_vec = 1 if sums else 2
        return add_terms(plan, lists, counts, envs, psis, sums, n_vec, sec_local, kind)

    plan = [(0, (0, 1)), (1, (0,))]
    away, home = added(plan, [lines[0], lines[1], lines_up[0]], None)
    (away,) = added([(3, (0,))], [lasts[0]], [away])
    (away,) = added([(2, (0,))], [lines_down[0]], [away], BF)
    arrived = over_mpo(away, FAR)
    (home,) = added([(2, (0,))], [lines_down[1]], [home])
    (home,) = added([(1, (0,)), (3, (0,))], [lines_up[1], lasts[1]], [home])
    return (home + arrived.astype(F32)).astype(BF)[:, None]


def solution(mesh):
    placed = (
        P("sec", None, None, None),
        P("mpo", "sec", None, None),
        P("mpo", "sec", None, None),
        P("mpo", "sec"),
        P("mpo", "sec"),
    )
    return jax.shard_map(
        per_device,
        mesh=mesh,
        in_specs=placed,
        out_specs=P("sec", "mpo", None, None),
        check_vma=False,
    )
```
